512 devices in a mesh: wide: 64 (over z, x_lo, core), narrow: 8 (over x_hi, y).
Axes of the slice: x: 4 (x_hi: 2, x_lo: 2; x = x_hi * 2 + x_lo), y: 4, z: 16, core: 2. Of those that a mesh axis runs over, the one named last changes fastest.
Arguments:
- b_blocks: bfloat16 [512, 1024, 1024], P(('wide', 'narrow')), may hold values from -6 to 6
- occ_energy: float32 [512], P(('wide', 'narrow')), may hold values from -1.2 to -0.4
- vir_energy: float32 [1024], replicated, may hold values from 0.2 to 3
- coef_vir: bfloat16 [1024, 1024], P('narrow'), may hold values from -3 to 3
Outputs:
- density: float32 [1024, 1024], P('wide', 'narrow')
- gamma_ao: bfloat16 [512, 1024, 1024], P('wide', 'narrow')
The draws below stay inside these ranges and needn't reach their ends.
All inputs are finite; a program needn't handle non-finite values.
Results may differ from the reference program's by a relative error of at most 0.015.
Values may be sent and summed in bfloat16 or wider, within the bound.
A program may use at most 64 MiB of HBM per device.

```python
import jax
import jax.numpy as jnp
from jax import lax

NV = 1024
NAUX = 1024
NAO = 1024
SLAB = 256
STEPS = 3
OCC = 512
N_WIDE = 64
N_NARROW = 8


def with_spikes(values, stream_key, source, target, shards_of, factor):
    def block_of(position):
        return (jnp.arange(values.shape[position]) // (values.shape[position] // shards_of)).reshape((-1,) + (1,) * (values.ndim - 1 - position))

    near = jax.random.permutation(stream_key, shards_of)[block_of(target)]
    far = (block_of(target) + shards_of // 2) % shards_of
    return jnp.where((block_of(source) == near) | (block_of(source) == far), factor * values, values)


def level_of(key, dims, cuts, low, top_value):
    def one(dim, blocks):
        steps = jax.random.uniform(jax.random.fold_in(jax.random.fold_in(key, 6), dim), (blocks,), jnp.float32, low / len(cuts), top_value / len(cuts))
        return jnp.repeat(jnp.exp(steps), dims[dim] // blocks).reshape((-1,) + (1,) * (len(dims) - dim - 1))

    loudness = one(*cuts[0])
    for cut in cuts[1:]:
        loudness = loudness * one(*cut)
    return loudness


def bell_draw(own_key, dims, width, limit, cuts=(), held_as=jnp.bfloat16):
    drawn = jax.random.normal(own_key, dims, jnp.float32) * width
    if len(cuts) > 0:
        drawn = level_of(own_key, dims, cuts, -0.22, 0.18) * drawn
    return jnp.clip(drawn, min=-limit, max=limit).astype(held_as)


def gaussian_with(stream_key, dims, spread, bound, split, heavy, kind=jnp.bfloat16):
    array = spread * jax.random.normal(stream_key, dims, jnp.float32)
    if split:
        array = array * level_of(stream_key, dims, split, -0.22, 0.18)
    return jnp.clip(with_spikes(array, jax.random.fold_in(stream_key, 3), *heavy), -bound, bound).astype(kind)


def setup_inputs(seed: int = 0) -> dict:
    key_list = jax.random.split(jax.random.key(seed), 5)
    return {
        "b_blocks": gaussian_with(key_list[0], (OCC, NV, NAUX), 0.15, 6.0, ((0, 512),), (0, 1, 512, 6.0)),
        "occ_energy": jnp.clip(-1.2 + 0.800000042 * jax.random.uniform(key_list[1], (OCC,), jnp.float32) ** level_of(key_list[1], (OCC,), ((0, 512),), -0.2, 0.2), -1.2, -0.4),
        "vir_energy": jnp.clip(jax.random.uniform(key_list[2], (NV,), jnp.float32, 0.2, 3.0), 0.2, 3.0),
        "coef_vir": bell_draw(key_list[3], (NAO, NV), 0.2, 3.0, ((0, 8),)),
    }


def reference(b_blocks, occ_energy, vir_energy, coef_vir):
    slab_count = NV // SLAB

    def one_orbital(dens, index):
        b_own = lax.dynamic_index_in_dim(b_blocks, index, 0, keepdims=False)
        e_own = lax.dynamic_slice_in_dim(occ_energy, index, 1)
        gamma = jnp.zeros((NV, NAUX), jnp.float32)
        for step in range(1, STEPS + 1):
            partner = (((index // N_NARROW - step) % N_WIDE) * N_NARROW + index % N_NARROW).astype(jnp.int32)
            start = ((step - 1) % slab_count) * SLAB
            slab = lax.dynamic_index_in_dim(b_blocks, partner, 0, keepdims=False)[start:start + SLAB]
            e_part = lax.dynamic_slice_in_dim(occ_energy, partner, 1)
            coupling = lax.dot_general(b_own, slab, (((1,), (1,)), ((), ())), preferred_element_type=jnp.float32)
            e_slab = vir_energy[start:start + SLAB]
            denom = (e_own + e_part) - vir_energy[:, None] - e_slab[None, :]
            amplitude = (coupling / denom).astype(jnp.bfloat16)
            gamma = gamma + jnp.dot(amplitude, slab, preferred_element_type=jnp.float32)
            dens = dens + lax.dot_general(amplitude, amplitude, (((1,), (1,)), ((), ())), preferred_element_type=jnp.float32)
        gamma_low = gamma.astype(jnp.bfloat16)
        out = jnp.dot(gamma_low.T, coef_vir.T, preferred_element_type=jnp.float32).astype(jnp.bfloat16)
        return dens, out

    dens, gamma_ao = lax.scan(one_orbital, jnp.zeros((NV, NV), jnp.float32), jnp.arange(OCC, dtype=jnp.int32))
    density = dens * (1.0 / (OCC * STEPS))
    return density, gamma_ao
```

```python
import jax
import jax.numpy as jnp
from jax import lax
from jax.experimental import pallas as pl
from jax.experimental.pallas import tpu as pltpu
from jax.sharding import PartitionSpec as P

NV = 1024
NAUX = 1024
NAO = 1024
SLAB = 256
STEPS = 3
PAIRS = 512 * STEPS
MESH = pl.DeviceIdType.MESH
BF = jnp.bfloat16
F32 = jnp.float32
NT = (((1,), (1,)), ((), ()))
Y_ORDER = (2, 1, 3, 0)


def kernel(
    b_hbm,
    occ_ref,
    vir_ref,
    coef_hbm,
    dens_ref,
    gao_ref,
    b_vm,
    slab,
    e_own,
    e_part,
    cf,
    vcol,
    amp,
    tr,
    st,
    d_own,
    d_send,
    d_recv,
    dy_send,
    dy_recv,
    dsum,
    dx_send,
    dx_recv,
    dz,
    dl_send,
    dl_recv,
    dg,
    dg_recv,
    o_send,
    local_sem,
    e_ss,
    e_rs,
    s_ss,
    s_rs,
    c_ss,
    c_rs,
    f_ss,
    f_rs,
    dc_ss,
    dc_rs,
    dy_ss,
    dy_rs,
    dx_ss,
    dx_rs,
    dl_ss,
    dl_rs,
    dg_ss,
    dg_rs,
    o_ss,
    o_rs,
):
    w = lax.axis_index("wide")
    n = lax.axis_index("narrow")
    z, xlo, core = w // 4, (w // 2) % 2, w % 2
    xhi, y = n // 4, n % 4
    g, l = z // 4, z % 4

    def at(z_, xlo_, core_, xhi_, y_):
        return (z_ * 4 + xlo_ * 2 + core_, xhi_ * 4 + y_)

    started = []

    def send(src, dst, ss, rs, dev):
        copy = pltpu.make_async_remote_copy(
            src_ref=src, dst_ref=dst, send_sem=ss, recv_sem=rs, device_id=dev, device_id_type=MESH
        )
        copy.start()
        started.append(copy)
        return copy

    other = at(z, xlo, 1 - core, xhi, y)
    across = at(z, 1 - xlo, core, 1 - xhi, y)
    ydev = [None] + [at(z, xlo, core, xhi, (y + d) % 4) for d in (1, 2, 3)]
    xdev = [
        at(z, xlo, core, 1 - xhi, y),
        at(z, 1 - xlo, core, xhi, y),
        across,
    ]
    ldev = [None] + [at(g * 4 + (l + d) % 4, xlo, core, xhi, y) for d in (1, 2, 3)]
    gdev = [None] + [at((g + d) % 4 * 4 + l, xlo, core, xhi, y) for d in (1, 2, 3)]

    barrier = pltpu.get_barrier_semaphore()
    greet = [((w + 64 - s) % 64, n) for s in (1, 2, 3)]
    greet += [other] + xdev + ydev[1:] + ldev[1:] + gdev[1:]
    greet += [at(z, xlo, core, 1 - xhi, (y + d) % 4) for d in (1, 2, 3)]
    for dev in greet:
        pl.semaphore_signal(barrier, inc=1, device_id=dev, device_id_type=MESH)

    load_b = pltpu.make_async_copy(b_hbm.at[0], b_vm, local_sem.at[0])
    load_b.start()
    load_c = pltpu.make_async_copy(coef_hbm, cf.at[n], local_sem.at[1])
    load_c.start()
    e_own[...] = jnp.full((8, 128), occ_ref[0], F32)

    pl.semaphore_wait(barrier, len(greet))

    e_cp, s_cp = [], []
    for s in range(STEPS):
        dev = ((w + s + 1) % 64, n)
        e_cp.append(send(e_own, e_part.at[s], e_ss.at[s], e_rs.at[s], dev))
    for s in range(STEPS):
        dev = ((w + s + 1) % 64, n)
        start = s % (NV // SLAB) * SLAB
        s_cp.append(send(b_hbm.at[0, pl.ds(start, SLAB)], slab.at[s], s_ss.at[s], s_rs.at[s], dev))

    half = pl.ds(pl.multiple_of(core * 64, 64), 64)
    mine = coef_hbm.at[half]
    c_cp = [send(mine, cf.at[n, half], c_ss.at[0], c_rs.at[0], across)]
    for d in (1, 2, 3):
        c_cp.append(send(mine, cf.at[n, half], c_ss.at[d], c_rs.at[d], ydev[d]))

    for k in range(8):
        row = vir_ref[:, k * 128 : (k + 1) * 128]
        vcol[k * 128 : (k + 1) * 128, :] = jnp.broadcast_to(row, (128, 128)).T

    c_cp[0].wait_recv()
    far = cf.at[(1 - xhi) * 4 + y, half]
    for d in (1, 2, 3):
        c_cp.append(send(far, far, c_ss.at[3 + d], c_rs.at[3 + d], ydev[d]))
    f_cp = [send(far, far, f_ss.at[0], f_rs.at[0], other)]
    for d in (1, 2, 3):
        c_cp[d].wait_recv()
        piece = cf.at[xhi * 4 + (y + 4 - d) % 4, half]
        f_cp.append(send(piece, piece, f_ss.at[d], f_rs.at[d], other))

    load_b.wait()

    def couple(s):
        e_cp[s].wait_recv()
        s_cp[s].wait_recv()
        start = s % (NV // SLAB) * SLAB
        e_sum = (e_own[...] + e_part[s])[0:1, 0:1]
        e_slab = vir_ref[:, start : start + SLAB]

        def rows(r, _):
            a = pl.ds(pl.multiple_of(r * 256, 256), 256)
            c = lax.dot_general(b_vm[a, :], slab[s], NT, preferred_element_type=F32)
            denom = (e_sum - vcol[a, 0:1]) - e_slab
            amp[a, s * SLAB : (s + 1) * SLAB] = (c / denom).astype(BF)
            return 0

        lax.fori_loop(0, 4, rows, 0)

    def transform(s):
        cols = slice(s * SLAB, (s + 1) * SLAB)
        for k in range(4):
            st[k * 256 : (k + 1) * 256, cols] = slab[s, :, k * 256 : (k + 1) * 256].T

        def rows(r, _):
            cc = cf[pl.ds(r * 2, 2)].reshape(256, NV)
            t = jnp.dot(cc, amp[:, cols], preferred_element_type=F32)
            tr[pl.ds(pl.multiple_of(r * 256, 256), 256), cols] = t.astype(BF)
            return 0

        lax.fori_loop(0, 4, rows, 0)

    couple(0)

    for d in (1, 2, 3):
        c_cp[3 + d].wait_recv()
        piece = cf.at[(1 - xhi) * 4 + (y + 4 - d) % 4, half]
        f_cp.append(send(piece, piece, f_ss.at[3 + d], f_rs.at[3 + d], other))
    load_c.wait()
    for copy in f_cp:
        copy.wait_recv()

    transform(0)
    couple(1)
    transform(1)
    couple(2)

    dc_cp = []
    for q, d in enumerate(Y_ORDER):
        y_ = (y + d) % 4
        lo = pl.ds(pl.multiple_of(y_ * 128, 128), 128)
        hi = pl.ds(pl.multiple_of(512 + y_ * 128, 128), 128)

        def rows(r, _):
            right = jnp.concatenate([amp[lo, :], amp[hi, :]], axis=0)
            a = pl.ds(pl.multiple_of(r * 256, 256), 256)
            v = lax.dot_general(amp[a, :], right, NT, preferred_element_type=F32)
            v = v.reshape(8, 2, 16, 256)
            v0, v1 = v[:, 0], v[:, 1]
            first = core == 0
            d_own[q, pl.ds(r * 8, 8)] = jnp.where(first, v0, v1)
            d_send[q, pl.ds(r * 8, 8)] = jnp.where(first, v1, v0).astype(BF)
            return 0

        lax.fori_loop(0, 4, rows, 0)
        dc_cp.append(send(d_send.at[q], d_recv.at[q], dc_ss.at[q], dc_rs.at[q], other))

    transform(2)

    dy_cp = []
    for q, d in enumerate(Y_ORDER):
        dc_cp[q].wait_recv()
        if d:

            def add(r, _):
                k = pl.ds(r * 8, 8)
                dy_send[q, k] = (d_own[q, k] + d_recv[q, k].astype(F32)).astype(BF)
                return 0

            lax.fori_loop(0, 4, add, 0)
            dy_cp.append(send(dy_send.at[q], dy_recv.at[q], dy_ss.at[q], dy_rs.at[q], ydev[d]))

    o_cp = []
    own_copy = None
    for q, d in enumerate(Y_ORDER):
        y_ = (y + d) % 4
        lo = pl.ds(pl.multiple_of(y_ * 128, 128), 128)
        hi = pl.ds(pl.multiple_of(512 + y_ * 128, 128), 128)

        def cols(k, _):
            left = jnp.concatenate([st[lo, :], st[hi, :]], axis=0)
            m = pl.ds(pl.multiple_of(k * 256, 256), 256)
            v = lax.dot_general(left, tr[m, :], NT, preferred_element_type=F32)
            v = v.astype(BF)
            o_send[q, 0, :, m] = v[:128]
            o_send[q, 1, :, m] = v[128:]
            return 0

        lax.fori_loop(0, 4, cols, 0)
        i = 2 * q
        o_cp.append(
            send(o_send.at[q, 1 - xhi], gao_ref.at[n], o_ss.at[i], o_rs.at[i], at(z, xlo, core, 1 - xhi, y_))
        )
        if d:
            o_cp.append(
                send(o_send.at[q, xhi], gao_ref.at[n], o_ss.at[i + 1], o_rs.at[i + 1], at(z, xlo, core, xhi, y_))
            )
        else:
            own_copy = pltpu.make_async_copy(o_send.at[q, xhi], gao_ref.at[n], local_sem.at[2])
            own_copy.start()

    for copy in dy_cp:
        copy.wait_recv()

    def sum_y(r, _):
        k = pl.ds(r * 8, 8)
        v = d_own[3, k] + d_recv[3, k].astype(F32)
        for q in range(3):
            v = v + dy_recv[q, k].astype(F32)
        v = v.reshape(4, 2, 16, 256)
        k4 = pl.ds(r * 4, 4)
        for lo_ in range(2):
            for hi_ in range(2):
                dsum[hi_, lo_, k4] = v[:, lo_, :, hi_ * 128 : (hi_ + 1) * 128]
        return 0

    lax.fori_loop(0, 4, sum_y, 0)
    dx_cp = []
    for k, (hi_, lo_) in enumerate(((1 - xhi, xlo), (xhi, 1 - xlo), (1 - xhi, 1 - xlo))):
        dx_send[k] = dsum[hi_, lo_].astype(BF)
        dx_cp.append(send(dx_send.at[k], dx_recv.at[k], dx_ss.at[k], dx_rs.at[k], xdev[k]))
    for copy in dx_cp:
        copy.wait_recv()
    v = dsum[xhi, xlo]
    for k in range(3):
        v = v + dx_recv[k].astype(F32)
    dz[...] = v.reshape(4, 4, 16, 128)
    dl_cp = []
    for d in (1, 2, 3):
        dl_send[d - 1] = dz[:, (l + d) % 4].astype(BF)
        dl_cp.append(send(dl_send.at[d - 1], dl_recv.at[d - 1], dl_ss.at[d - 1], dl_rs.at[d - 1], ldev[d]))
    for copy in dl_cp:
        copy.wait_recv()
    v = dz[:, l]
    for k in range(3):
        v = v + dl_recv[k].astype(F32)
    dg[...] = v
    dg_cp = []
    for d in (1, 2, 3):
        dg_cp.append(send(dg.at[(g + d) % 4], dg_recv.at[d - 1], dg_ss.at[d - 1], dg_rs.at[d - 1], gdev[d]))
    for copy in dg_cp:
        copy.wait_recv()
    v = dg[g]
    for k in range(3):
        v = v + dg_recv[k]
    dens_ref[...] = v * (1.0 / PAIRS)

    own_copy.wait()
    for copy in o_cp:
        copy.wait_recv()
    for copy in started:
        copy.wait_send()


def on_device(b_blocks, occ_energy, vir_energy, coef_vir):
    dma = pltpu.SemaphoreType.DMA
    vm = pltpu.VMEM
    scratch = [
        vm((NV, NAUX), BF),
        vm((STEPS, SLAB, NAUX), BF),
        vm((8, 128), F32),
        vm((STEPS, 8, 128), F32),
        vm((8, 128, NV), BF),
        vm((NV, 128), F32),
        vm((NV, STEPS * SLAB), BF),
        vm((NAO, STEPS * SLAB), BF),
        vm((NAUX, STEPS * SLAB), BF),
        vm((4, 32, 16, 256), F32),
        vm((4, 32, 16, 256), BF),
        vm((4, 32, 16, 256), BF),
        vm((3, 32, 16, 256), BF),
        vm((3, 32, 16, 256), BF),
        vm((2, 2, 16, 16, 128), F32),
        vm((3, 16, 16, 128), BF),
        vm((3, 16, 16, 128), BF),
        vm((4, 4, 16, 128), F32),
        vm((3, 4, 16, 128), BF),
        vm((3, 4, 16, 128), BF),
        vm((4, 16, 128), F32),
        vm((3, 16, 128), F32),
        vm((4, 2, 128, NAO), BF),
        dma((3,)),
    ]
    for count in (3, 3, 7, 7, 4, 3, 3, 3, 3, 8):
        scratch += [dma((count,)), dma((count,))]
    return pl.pallas_call(
        kernel,
        out_shape=(
            jax.ShapeDtypeStruct((16, 128), F32),
            jax.ShapeDtypeStruct((8, 128, NAO), BF),
        ),
        in_specs=[
            pl.BlockSpec(memory_space=pl.ANY),
            pl.BlockSpec(memory_space=pltpu.SMEM),
            pl.BlockSpec(memory_space=pltpu.VMEM),
            pl.BlockSpec(memory_space=pl.ANY),
        ],
        out_specs=(
            pl.BlockSpec(memory_space=pltpu.VMEM),
            pl.BlockSpec(memory_space=pl.ANY),
        ),
        scratch_shapes=scratch,
        compiler_params=pltpu.CompilerParams(
            collective_id=0, has_side_effects=True, vmem_limit_bytes=48 * 1024 * 1024
        ),
    )(b_blocks, occ_energy, vir_energy.reshape(1, NV), coef_vir)


def solution(mesh):
    return jax.shard_map(
        on_device,
        mesh=mesh,
        in_specs=(P(("wide", "narrow"), None, None), P(("wide", "narrow")), P(), P("narrow", None)),
        out_specs=(P("wide", "narrow"), P("wide", "narrow", None)),
        check_vma=False,
    )
```

```python
import jax
import jax.numpy as jnp
from jax import lax
from jax.experimental import pallas as pl
from jax.experimental.pallas import tpu as pltpu
from jax.sharding import PartitionSpec as P

NV = 1024
NAUX = 1024
NAO = 1024
SLAB = 256
STEPS = 3
PAIRS = 512 * STEPS
MESH = pl.DeviceIdType.MESH
BF = jnp.bfloat16
F32 = jnp.float32
NT = (((1,), (1,)), ((), ()))
Y_ORDER = (2, 1, 3, 0)


def kernel(
    b_hbm,
    occ_ref,
    vir_hbm,
    coef_hbm,
    dens_ref,
    gao_ref,
    b_vm,
    slab,
    e_own,
    e_part,
    cf,
    vcol,
    amp,
    tr,
    st,
    d_own,
    d_send,
    d_recv,
    y1_send,
    y1_recv,
    x1_send,
    x1_recv,
    e0,
    e1,
    x2_send,
    x2_recv,
    y2_send,
    y2_recv,
    dz,
    dl_send,
    dl_recv,
    dg,
    dg_recv,
    vir_ref,
    o_send,
    d_acc,
    word,
    local_sem,
    e_ss,
    e_rs,
    s_ss,
    s_rs,
    c_ss,
    c_rs,
    f_ss,
    f_rs,
    dc_ss,
    dc_rs,
    y1_ss,
    y1_rs,
    x1_ss,
    x1_rs,
    x2_ss,
    x2_rs,
    y2_ss,
    y2_rs,
    dl_ss,
    dl_rs,
    dg_ss,
    dg_rs,
    o_ss,
    o_rs,
    r_ss,
    r_rs,
):
    w = lax.axis_index("wide")
    n = lax.axis_index("narrow")
    z, xlo, core = w // 4, (w // 2) % 2, w % 2
    xhi, y = n // 4, n % 4
    g, l = z // 4, z % 4

    def at(z_, xlo_, core_, xhi_, y_):
        return (z_ * 4 + xlo_ * 2 + core_, xhi_ * 4 + y_)

    started = []

    def send(src, dst, ss, rs, dev):
        copy = pltpu.make_async_remote_copy(
            src_ref=src, dst_ref=dst, send_sem=ss, recv_sem=rs, device_id=dev, device_id_type=MESH
        )
        copy.start()
        started.append(copy)
        return copy

    other = at(z, xlo, 1 - core, xhi, y)
    across = at(z, 1 - xlo, core, 1 - xhi, y)
    ydev = [None] + [at(z, xlo, core, xhi, (y + d) % 4) for d in (1, 2, 3)]
    xdev = [
        at(z, xlo, core, 1 - xhi, y),
        at(z, 1 - xlo, core, xhi, y),
        across,
    ]
    ldev = [None] + [at(g * 4 + (l + d) % 4, xlo, core, xhi, y) for d in (1, 2, 3)]
    gdev = [None] + [at((g + d) % 4 * 4 + l, xlo, core, xhi, y) for d in (1, 2, 3)]

    barrier = pltpu.get_barrier_semaphore()
    greet = [((w + 64 - s) % 64, n) for s in (1, 2, 3, 4)]
    greet += [((w + 2) % 64, n), ((w + 4) % 64, n)]
    greet += [other] + xdev + ydev[1:]
    for dev in greet:
        pl.semaphore_signal(barrier, inc=1, device_id=dev, device_id_type=MESH)

    load_b = pltpu.make_async_copy(b_hbm.at[0], b_vm, local_sem.at[0])
    load_b.start()
    load_c = pltpu.make_async_copy(coef_hbm, cf.at[n], local_sem.at[1])
    load_c.start()
    load_v = pltpu.make_async_copy(vir_hbm, vir_ref, local_sem.at[3])
    load_v.start()
    e_own[...] = jnp.full((8, 128), occ_ref[0], F32)

    pl.semaphore_wait(barrier, len(greet))

    def pass_word(k, devs):
        for dev in devs:
            pl.semaphore_signal(word.at[k], inc=1, device_id=dev, device_id_type=MESH)

    def along(d):
        return [((w + 4 * d) % 64, n), ((w + 64 - 4 * d) % 64, n)]

    e_cp = []
    for s in range(STEPS):
        dev = ((w + s + 1) % 64, n)
        e_cp.append(send(e_own, e_part.at[s], e_ss.at[s], e_rs.at[s], dev))
    s_early, s_late = core * 2, 2 - core * 2
    r_early, r_late = 2 - core * 2, core * 2

    def slab_copy(s):
        return pltpu.make_async_remote_copy(
            src_ref=b_hbm.at[0, pl.ds(pl.multiple_of(s * SLAB, SLAB), SLAB)],
            dst_ref=slab.at[s],
            send_sem=s_ss.at[s],
            recv_sem=s_rs.at[s],
            device_id=((w + s + 1) % 64, n),
            device_id_type=MESH,
        )

    def quarter(k):
        return pltpu.make_async_remote_copy(
            src_ref=b_hbm.at[0, pl.ds(SLAB + k * 64, 64)],
            dst_ref=slab.at[1, pl.ds(k * 64, 64)],
            send_sem=r_ss.at[k],
            recv_sem=r_rs.at[4 + k],
            device_id=((w + 2) % 64, n),
            device_id_type=MESH,
        )

    for k in range(4):
        quarter(k).start()

    slab_copy(s_early).start()
    slab_copy(s_late).start()
    pass_word(0, along(1))
    pass_word(3, [xdev[0]])

    half = pl.ds(pl.multiple_of(core * 64, 64), 64)
    mine = coef_hbm.at[half]
    c_cp = [send(mine, cf.at[n, half], c_ss.at[0], c_rs.at[0], across)]
    for d in (1, 2, 3):
        c_cp.append(send(mine, cf.at[n, half], c_ss.at[d], c_rs.at[d], ydev[d]))

    load_v.wait()
    for k in range(8):
        row = vir_ref[:, k * 128 : (k + 1) * 128]
        vcol[k * 128 : (k + 1) * 128, :] = jnp.broadcast_to(row, (128, 128)).T

    c_cp[0].wait_recv()
    far = cf.at[(1 - xhi) * 4 + y, half]
    for d in (1, 2, 3):
        c_cp.append(send(far, far, c_ss.at[3 + d], c_rs.at[3 + d], ydev[d]))
    f_cp = [send(far, far, f_ss.at[0], f_rs.at[0], other)]
    pl.semaphore_wait(word.at[0], 2)
    pass_word(1, along(2))
    for d in (1, 2, 3):
        c_cp[d].wait_recv()
        piece = cf.at[xhi * 4 + (y + 4 - d) % 4, half]
        f_cp.append(send(piece, piece, f_ss.at[d], f_rs.at[d], other))
    pl.semaphore_wait(word.at[1], 2)
    pass_word(2, along(4))
    load_b.wait()

    def couple(slot, s):
        if slot == 0:
            for copy in e_cp:
                copy.wait_recv()
        if slot == 1:
            for k in range(4):
                quarter(k).wait_recv()
        else:
            slab_copy(s).wait_recv()
        e_sum = (e_own[...] + e_part[s])[0:1, 0:1]
        e_slab = vir_ref[:, pl.ds(pl.multiple_of(s * SLAB, SLAB), SLAB)]
        c = lax.dot_general(b_vm[...], slab[s], NT, preferred_element_type=F32)
        denom = (e_sum - vcol[:, 0:1]) - e_slab
        amp[:, slot * SLAB : (slot + 1) * SLAB] = (c / denom).astype(BF)

    def transform(slot, s):
        cols = slice(slot * SLAB, (slot + 1) * SLAB)
        for k in range(4):
            st[k * 256 : (k + 1) * 256, cols] = slab[s, :, k * 256 : (k + 1) * 256].T

        t = jnp.dot(cf[...].reshape(NAO, NV), amp[:, cols], preferred_element_type=F32)
        tr[:, cols] = t.astype(BF)

    couple(0, r_early)

    for d in (1, 2, 3):
        c_cp[3 + d].wait_recv()
        piece = cf.at[(1 - xhi) * 4 + (y + 4 - d) % 4, half]
        f_cp.append(send(piece, piece, f_ss.at[3 + d], f_rs.at[3 + d], other))
    load_c.wait()
    for copy in f_cp:
        copy.wait_recv()

    transform(0, r_early)
    couple(1, 1)
    transform(1, 1)

    def columns(d):
        y_ = (y + d) % 4
        return (y_, pl.ds(pl.multiple_of(y_ * 128, 128), 128), pl.ds(pl.multiple_of(512 + y_ * 128, 128), 128))

    for q, d in enumerate(Y_ORDER):
        _, lo, hi = columns(d)
        right = jnp.concatenate([amp[lo, : 2 * SLAB], amp[hi, : 2 * SLAB]], axis=0)
        d_acc[q] = lax.dot_general(amp[:, : 2 * SLAB], right, NT, preferred_element_type=F32)
    couple(2, r_late)

    top, low = pl.ds(8, 8), pl.ds(0, 8)
    dt_cp, dc_cp = [], []
    for q, d in enumerate(Y_ORDER):
        y_, lo, hi = columns(d)
        right = jnp.concatenate([amp[lo, 2 * SLAB :], amp[hi, 2 * SLAB :]], axis=0)
        v = d_acc[q] + lax.dot_general(amp[:, 2 * SLAB :], right, NT, preferred_element_type=F32)
        v = v.reshape(16, 2, 2, 16, 256)
        v0, v1 = v[:, :, 0], v[:, :, 1]
        keep = jnp.where(core == 0, v0, v1)
        give = jnp.where(core == 0, v1, v0).astype(BF)
        for h in range(2):
            for x_ in range(2):
                d_own[y_, h, x_] = keep[:, x_, :, h * 128 : (h + 1) * 128]
                d_send[y_, h, x_] = give[:, x_, :, h * 128 : (h + 1) * 128]
        i = 2 * q
        dt_cp.append(send(d_send.at[y_, :, :, top], d_recv.at[y_, :, :, top], dc_ss.at[i], dc_rs.at[i], other))
        i = i + 1
        dc_cp.append(send(d_send.at[y_, :, :, low], d_recv.at[y_, :, :, low], dc_ss.at[i], dc_rs.at[i], other))

    transform(2, r_late)

    for copy in dt_cp:
        copy.wait_recv()
    xs = ((1 - xhi, xlo), (xhi, 1 - xlo), (1 - xhi, 1 - xlo))
    x1_cp, y1_cp = [], []
    for k, (h, x_) in enumerate(xs):

        def add(r, _):
            v = d_own[r, h, x_, top] + d_recv[r, h, x_, top].astype(F32)
            x1_send[k, r] = v.astype(BF)
            return 0

        lax.fori_loop(0, 4, add, 0)
        x1_cp.append(send(x1_send.at[k], x1_recv.at[k], x1_ss.at[k], x1_rs.at[k], xdev[k]))
    for q, d in enumerate(Y_ORDER):
        dc_cp[q].wait_recv()
        if d:

            def add(r, _):
                h, x_ = r // 2, r % 2
                v = d_own[(y + d) % 4, h, x_, low] + d_recv[(y + d) % 4, h, x_, low].astype(F32)
                y1_send[q, h, x_] = v.astype(BF)
                return 0

            lax.fori_loop(0, 4, add, 0)
            y1_cp.append(send(y1_send.at[q], y1_recv.at[q], y1_ss.at[q], y1_rs.at[q], ydev[d]))

    pl.semaphore_wait(word.at[3], 1)
    o_cp = []

    def blocks(q):
        d = Y_ORDER[q]
        y_, lo, hi = columns(d)
        left = jnp.concatenate([st[lo, :], st[hi, :]], axis=0)
        v = lax.dot_general(left, tr[...], NT, preferred_element_type=F32).astype(BF)
        o_send[q, 0] = v[:128]
        o_send[q, 1] = v[128:]
        i = 2 * q
        o_cp.append(
            send(o_send.at[q, 1 - xhi], gao_ref.at[n], o_ss.at[i], o_rs.at[i], at(z, xlo, core, 1 - xhi, y_))
        )
        if d:
            i = i + 1
            o_cp.append(send(o_send.at[q, xhi], gao_ref.at[n], o_ss.at[i], o_rs.at[i], at(z, xlo, core, xhi, y_)))

    blocks(0)
    blocks(1)
    for copy in x1_cp:
        copy.wait_recv()

    def sum_x(r, _):
        v = d_own[r, xhi, xlo, top] + d_recv[r, xhi, xlo, top].astype(F32)
        for k in range(3):
            v = v + x1_recv[k, r].astype(F32)
        e1[r] = v
        return 0

    lax.fori_loop(0, 4, sum_x, 0)
    y2_cp = []
    for d in (1, 2, 3):
        y2_send[d - 1] = e1[(y + d) % 4].astype(BF)
        y2_cp.append(send(y2_send.at[d - 1], y2_recv.at[d - 1], y2_ss.at[d - 1], y2_rs.at[d - 1], ydev[d]))
    for copy in y1_cp:
        copy.wait_recv()

    def sum_y(r, _):
        h, x_ = r // 2, r % 2
        v = d_own[y, h, x_, low] + d_recv[y, h, x_, low].astype(F32)
        for k in range(3):
            v = v + y1_recv[k, h, x_].astype(F32)
        e0[h, x_] = v
        return 0

    lax.fori_loop(0, 4, sum_y, 0)
    x2_cp = []
    for k, (h, x_) in enumerate(xs):
        x2_send[k] = e0[h, x_].astype(BF)
        x2_cp.append(send(x2_send.at[k], x2_recv.at[k], x2_ss.at[k], x2_rs.at[k], xdev[k]))
    blocks(2)
    for copy in y2_cp + x2_cp:
        copy.wait_recv()
    v0, v1 = e0[xhi, xlo], e1[y]
    for k in range(3):
        v0 = v0 + x2_recv[k].astype(F32)
        v1 = v1 + y2_recv[k].astype(F32)
    dz[0:2] = v0.reshape(2, 4, 16, 128)
    dz[2:4] = v1.reshape(2, 4, 16, 128)
    pl.semaphore_wait(word.at[2], 2)
    dl_cp = []
    for d in (1, 2, 3):
        dl_send[d - 1] = dz[:, (l + d) % 4].astype(BF)
        dl_cp.append(send(dl_send.at[d - 1], dl_recv.at[d - 1], dl_ss.at[d - 1], dl_rs.at[d - 1], ldev[d]))
    blocks(3)
    own_copy = pltpu.make_async_copy(o_send.at[3, xhi], gao_ref.at[n], local_sem.at[2])
    own_copy.start()
    for copy in dl_cp:
        copy.wait_recv()
    v = dz[:, l]
    for k in range(3):
        v = v + dl_recv[k].astype(F32)
    dg[...] = v
    dg_cp = []
    for d in (1, 2, 3):
        dg_cp.append(send(dg.at[(g + d) % 4], dg_recv.at[d - 1], dg_ss.at[d - 1], dg_rs.at[d - 1], gdev[d]))
    for copy in dg_cp:
        copy.wait_recv()
    v = dg[g]
    for k in range(3):
        v = v + dg_recv[k]
    dens_ref[...] = v * (1.0 / PAIRS)

    own_copy.wait()
    for copy in o_cp:
        copy.wait_recv()
    for copy in started:
        copy.wait_send()

    slab_copy(s_early).wait_send()
    slab_copy(s_late).wait_send()
    for k in range(4):
        quarter(k).wait_send()


def on_device(b_blocks, occ_energy, vir_energy, coef_vir):
    dma = pltpu.SemaphoreType.DMA
    vm = pltpu.VMEM
    scratch = [
        vm((NV, NAUX), BF),
        vm((STEPS, SLAB, NAUX), BF),
        vm((8, 128), F32),
        vm((STEPS, 8, 128), F32),
        vm((8, 128, NV), BF),
        vm((NV, 128), F32),
        vm((NV, STEPS * SLAB), BF),
        vm((NAO, STEPS * SLAB), BF),
        vm((NAUX, STEPS * SLAB), BF),
        vm((4, 2, 2, 16, 16, 128), F32),
        vm((4, 2, 2, 16, 16, 128), BF),
        vm((4, 2, 2, 16, 16, 128), BF),
        vm((3, 2, 2, 8, 16, 128), BF),
        vm((3, 2, 2, 8, 16, 128), BF),
        vm((3, 4, 8, 16, 128), BF),
        vm((3, 4, 8, 16, 128), BF),
        vm((2, 2, 8, 16, 128), F32),
        vm((4, 8, 16, 128), F32),
        vm((3, 8, 16, 128), BF),
        vm((3, 8, 16, 128), BF),
        vm((3, 8, 16, 128), BF),
        vm((3, 8, 16, 128), BF),
        vm((4, 4, 16, 128), F32),
        vm((3, 4, 16, 128), BF),
        vm((3, 4, 16, 128), BF),
        vm((4, 16, 128), F32),
        vm((3, 16, 128), F32),
        vm((1, NV), F32),
        vm((4, 2, 128, NAO), BF),
        vm((4, NV, 256), F32),
        pltpu.SemaphoreType.REGULAR((4,)),
        dma((4,)),
    ]
    for count in (3, 3, 7, 7, 8, 3, 3, 3, 3, 3, 3, 8, 8):
        scratch += [dma((count,)), dma((count,))]
    return pl.pallas_call(
        kernel,
        out_shape=(
            jax.ShapeDtypeStruct((16, 128), F32),
            jax.ShapeDtypeStruct((8, 128, NAO), BF),
        ),
        in_specs=[
            pl.BlockSpec(memory_space=pltpu.HBM),
            pl.BlockSpec(memory_space=pltpu.SMEM),
            pl.BlockSpec(memory_space=pltpu.HBM),
            pl.BlockSpec(memory_space=pltpu.HBM),
        ],
        out_specs=(
            pl.BlockSpec(memory_space=pltpu.VMEM),
            pl.BlockSpec(memory_space=pl.ANY),
        ),
        scratch_shapes=scratch,
        compiler_params=pltpu.CompilerParams(
            collective_id=0, has_side_effects=True, vmem_limit_bytes=50 * 1024 * 1024
        ),
    )(b_blocks, occ_energy, vir_energy.reshape(1, NV), coef_vir)


def solution(mesh):
    return jax.shard_map(
        on_device,
        mesh=mesh,
        in_specs=(P(("wide", "narrow"), None, None), P(("wide", "narrow")), P(), P("narrow", None)),
        out_specs=(P("wide", "narrow"), P("wide", "narrow", None)),
        check_vma=False,
    )
```

```python
import jax
import jax.numpy as jnp
from jax import lax
from jax.experimental import pallas as pl
from jax.experimental.pallas import tpu as pltpu
from jax.sharding import PartitionSpec as P

NV = 1024
NAUX = 1024
NAO = 1024
SLAB = 256
STEPS = 3
PAIRS = 512 * STEPS
MESH = pl.DeviceIdType.MESH
BF = jnp.bfloat16
F32 = jnp.float32
NT = (((1,), (1,)), ((), ()))
Y_ORDER = (2, 1, 3, 0)


def kernel(
    b_hbm,
    occ_ref,
    vir_hbm,
    coef_hbm,
    dens_ref,
    gao_ref,
    b_vm,
    slab,
    e_own,
    e_part,
    cf,
    vcol,
    amp,
    tr,
    st,
    d_own,
    d_send,
    d_recv,
    zp_send,
    zp_recv,
    y1_send,
    y1_recv,
    x1_send,
    x1_recv,
    e0,
    e1,
    x2_send,
    x2_recv,
    y2_send,
    y2_recv,
    dz,
    dl_send,
    dl_recv,
    dg,
    dg_recv,
    vir_ref,
    o_send,
    d_acc,
    word,
    local_sem,
    e_ss,
    e_rs,
    s_ss,
    s_rs,
    c_ss,
    c_rs,
    f_ss,
    f_rs,
    dc_ss,
    dc_rs,
    zp_ss,
    zp_rs,
    y1_ss,
    y1_rs,
    x1_ss,
    x1_rs,
    x2_ss,
    x2_rs,
    y2_ss,
    y2_rs,
    dl_ss,
    dl_rs,
    dg_ss,
    dg_rs,
    o_ss,
    o_rs,
    r_ss,
    r_rs,
):
    w = lax.axis_index("wide")
    n = lax.axis_index("narrow")
    z, xlo, core = w // 4, (w // 2) % 2, w % 2
    xhi, y = n // 4, n % 4
    g, l = z // 4, z % 4

    def at(z_, xlo_, core_, xhi_, y_):
        return (z_ * 4 + xlo_ * 2 + core_, xhi_ * 4 + y_)

    started = []

    def send(src, dst, ss, rs, dev):
        copy = pltpu.make_async_remote_copy(
            src_ref=src, dst_ref=dst, send_sem=ss, recv_sem=rs, device_id=dev, device_id_type=MESH
        )
        copy.start()
        started.append(copy)
        return copy

    other = at(z, xlo, 1 - core, xhi, y)
    across = at(z, 1 - xlo, core, 1 - xhi, y)
    ydev = [None] + [at(z, xlo, core, xhi, (y + d) % 4) for d in (1, 2, 3)]
    xdev = [
        at(z, xlo, core, 1 - xhi, y),
        at(z, 1 - xlo, core, xhi, y),
        across,
    ]
    ldev = [None] + [at(g * 4 + (l + d) % 4, xlo, core, xhi, y) for d in (1, 2, 3)]
    gdev = [None] + [at((g + d) % 4 * 4 + l, xlo, core, xhi, y) for d in (1, 2, 3)]

    barrier = pltpu.get_barrier_semaphore()
    greet = [((w + 64 - s) % 64, n) for s in (1, 2, 3, 4)]
    greet += [((w + 2) % 64, n), ((w + 4) % 64, n)]
    greet += [other] + xdev + ydev[1:]
    for dev in greet:
        pl.semaphore_signal(barrier, inc=1, device_id=dev, device_id_type=MESH)

    load_b = pltpu.make_async_copy(b_hbm.at[0], b_vm, local_sem.at[0])
    load_b.start()
    load_c = pltpu.make_async_copy(coef_hbm, cf.at[n], local_sem.at[1])
    load_c.start()
    load_v = pltpu.make_async_copy(vir_hbm, vir_ref, local_sem.at[3])
    load_v.start()
    e_own[...] = jnp.full((8, 128), occ_ref[0], F32)

    pl.semaphore_wait(barrier, len(greet))

    def pass_word(k, devs):
        for dev in devs:
            pl.semaphore_signal(word.at[k], inc=1, device_id=dev, device_id_type=MESH)

    def along(d):
        return [((w + 4 * d) % 64, n), ((w + 64 - 4 * d) % 64, n)]

    e_cp = []
    for s in range(STEPS):
        dev = ((w + s + 1) % 64, n)
        e_cp.append(send(e_own, e_part.at[s], e_ss.at[s], e_rs.at[s], dev))
    s_early, s_late = core * 2, 2 - core * 2
    r_early, r_late = 2 - core * 2, core * 2

    def slab_copy(s):
        return pltpu.make_async_remote_copy(
            src_ref=b_hbm.at[0, pl.ds(pl.multiple_of(s * SLAB, SLAB), SLAB)],
            dst_ref=slab.at[s],
            send_sem=s_ss.at[s],
            recv_sem=s_rs.at[s],
            device_id=((w + s + 1) % 64, n),
            device_id_type=MESH,
        )

    def quarter(k):
        return pltpu.make_async_remote_copy(
            src_ref=b_hbm.at[0, pl.ds(SLAB + k * 64, 64)],
            dst_ref=slab.at[1, pl.ds(k * 64, 64)],
            send_sem=r_ss.at[k],
            recv_sem=r_rs.at[4 + k],
            device_id=((w + 2) % 64, n),
            device_id_type=MESH,
        )

    for k in range(4):
        quarter(k).start()

    slab_copy(s_early).start()
    slab_copy(s_late).start()
    pass_word(0, along(1))
    pass_word(3, [xdev[0]])

    half = pl.ds(pl.multiple_of(core * 64, 64), 64)
    mine = coef_hbm.at[half]
    c_cp = [send(mine, cf.at[n, half], c_ss.at[0], c_rs.at[0], across)]
    for d in (1, 2, 3):
        c_cp.append(send(mine, cf.at[n, half], c_ss.at[d], c_rs.at[d], ydev[d]))

    load_v.wait()
    for k in range(8):
        row = vir_ref[:, k * 128 : (k + 1) * 128]
        vcol[k * 128 : (k + 1) * 128, :] = jnp.broadcast_to(row, (128, 128)).T

    c_cp[0].wait_recv()
    far = cf.at[(1 - xhi) * 4 + y, half]
    for d in (1, 2, 3):
        c_cp.append(send(far, far, c_ss.at[3 + d], c_rs.at[3 + d], ydev[d]))
    f_cp = [send(far, far, f_ss.at[0], f_rs.at[0], other)]
    pl.semaphore_wait(word.at[0], 2)
    pass_word(1, along(2))
    for d in (1, 2, 3):
        c_cp[d].wait_recv()
        piece = cf.at[xhi * 4 + (y + 4 - d) % 4, half]
        f_cp.append(send(piece, piece, f_ss.at[d], f_rs.at[d], other))
    pl.semaphore_wait(word.at[1], 2)
    pass_word(2, along(4))
    load_b.wait()

    def couple(slot, s):
        if slot == 0:
            for copy in e_cp:
                copy.wait_recv()
        if slot == 1:
            for k in range(4):
                quarter(k).wait_recv()
        else:
            slab_copy(s).wait_recv()
        e_sum = (e_own[...] + e_part[s])[0:1, 0:1]
        e_slab = vir_ref[:, pl.ds(pl.multiple_of(s * SLAB, SLAB), SLAB)]
        c = lax.dot_general(b_vm[...], slab[s], NT, preferred_element_type=F32)
        denom = (e_sum - vcol[:, 0:1]) - e_slab
        amp[:, slot * SLAB : (slot + 1) * SLAB] = (c / denom).astype(BF)

    def transform(slot, s):
        cols = slice(slot * SLAB, (slot + 1) * SLAB)
        for k in range(4):
            st[k * 256 : (k + 1) * 256, cols] = slab[s, :, k * 256 : (k + 1) * 256].T

        t = jnp.dot(cf[...].reshape(NAO, NV), amp[:, cols], preferred_element_type=F32)
        tr[:, cols] = t.astype(BF)

    couple(0, r_early)

    for d in (1, 2, 3):
        c_cp[3 + d].wait_recv()
        piece = cf.at[(1 - xhi) * 4 + (y + 4 - d) % 4, half]
        f_cp.append(send(piece, piece, f_ss.at[3 + d], f_rs.at[3 + d], other))
    load_c.wait()
    for copy in f_cp:
        copy.wait_recv()

    transform(0, r_early)
    couple(1, 1)
    transform(1, 1)

    def columns(d):
        y_ = (y + d) % 4
        return (y_, pl.ds(pl.multiple_of(y_ * 128, 128), 128), pl.ds(pl.multiple_of(512 + y_ * 128, 128), 128))

    for q, d in enumerate(Y_ORDER):
        _, lo, hi = columns(d)
        right = jnp.concatenate([amp[lo, : 2 * SLAB], amp[hi, : 2 * SLAB]], axis=0)
        d_acc[q] = lax.dot_general(amp[:, : 2 * SLAB], right, NT, preferred_element_type=F32)
    couple(2, r_late)

    transform(2, r_late)
    pl.semaphore_wait(word.at[3], 1)
    o_cp = []

    def blocks(q):
        d = Y_ORDER[q]
        y_, lo, hi = columns(d)
        left = jnp.concatenate([st[lo, :], st[hi, :]], axis=0)
        v = lax.dot_general(left, tr[...], NT, preferred_element_type=F32).astype(BF)
        o_send[q, 0] = v[:128]
        o_send[q, 1] = v[128:]
        i = 2 * q
        o_cp.append(
            send(o_send.at[q, 1 - xhi], gao_ref.at[n], o_ss.at[i], o_rs.at[i], at(z, xlo, core, 1 - xhi, y_))
        )
        if d:
            i = i + 1
            o_cp.append(send(o_send.at[q, xhi], gao_ref.at[n], o_ss.at[i], o_rs.at[i], at(z, xlo, core, xhi, y_)))

    for q in range(4):
        blocks(q)
    own_copy = pltpu.make_async_copy(o_send.at[3, xhi], gao_ref.at[n], local_sem.at[2])
    own_copy.start()
    top, low = pl.ds(4, 4), pl.ds(0, 4)
    par = z % 2
    dt_cp, dc_cp = [], []
    for q, d in enumerate(Y_ORDER):
        y_, lo, hi = columns(d)
        right = jnp.concatenate([amp[lo, 2 * SLAB :], amp[hi, 2 * SLAB :]], axis=0)
        v = d_acc[q] + lax.dot_general(amp[:, 2 * SLAB :], right, NT, preferred_element_type=F32)
        v = v.reshape(8, 2, 2, 2, 16, 256)
        v0, v1 = v[:, :, :, 0], v[:, :, :, 1]
        keep = jnp.where(core == 0, v0, v1)
        give = jnp.where(core == 0, v1, v0).astype(BF)
        for h in range(2):
            for x_ in range(2):
                for p in range(2):
                    d_own[y_, h, x_, p] = keep[:, p, x_, :, h * 128 : (h + 1) * 128]
                    d_send[y_, h, x_, p] = give[:, p, x_, :, h * 128 : (h + 1) * 128]
        for i, p, cps in ((2 * q, 1 - par, dt_cp), (2 * q + 1, par, dc_cp)):
            cps.append(send(d_send.at[y_, :, :, p], d_recv.at[y_, :, :, p], dc_ss.at[i], dc_rs.at[i], other))


    for copy in dt_cp:
        copy.wait_recv()
    step = 1 - 2 * par
    zdev = [((w + 64 + 4 * step) % 64, n), ((w + 64 - 4 * step) % 64, n)]
    zp_cp = []
    for k in range(2):

        def add(r, _):
            h, x_ = r // 2, r % 2
            for i in range(2):
                v = d_own[2 * k + i, h, x_, 1 - par] + d_recv[2 * k + i, h, x_, 1 - par].astype(F32)
                zp_send[k, i, h, x_] = v.astype(BF)
            return 0

        lax.fori_loop(0, 4, add, 0)
        zp_cp.append(send(zp_send.at[k], zp_recv.at[k], zp_ss.at[k], zp_rs.at[k], zdev[k]))

    for copy in dc_cp + zp_cp:
        copy.wait_recv()

    def have(y_, h, x_, part):
        v = d_own[y_, h, x_, par, part] + d_recv[y_, h, x_, par, part].astype(F32)
        return v + zp_recv[y_ // 2, y_ % 2, h, x_, part].astype(F32)

    xs = ((1 - xhi, xlo), (xhi, 1 - xlo), (1 - xhi, 1 - xlo))
    x1_cp, y1_cp = [], []
    for k, (h, x_) in enumerate(xs):

        def add(r, _):
            x1_send[k, r] = have(r, h, x_, top).astype(BF)
            return 0

        lax.fori_loop(0, 4, add, 0)
        x1_cp.append(send(x1_send.at[k], x1_recv.at[k], x1_ss.at[k], x1_rs.at[k], xdev[k]))
    for q, d in enumerate(Y_ORDER[:3]):

        def add(r, _):
            y1_send[q, r // 2, r % 2] = have((y + d) % 4, r // 2, r % 2, low).astype(BF)
            return 0

        lax.fori_loop(0, 4, add, 0)
        y1_cp.append(send(y1_send.at[q], y1_recv.at[q], y1_ss.at[q], y1_rs.at[q], ydev[d]))

    for copy in x1_cp:
        copy.wait_recv()

    def sum_x(r, _):
        v = have(r, xhi, xlo, top)
        for k in range(3):
            v = v + x1_recv[k, r].astype(F32)
        e1[r] = v
        return 0

    lax.fori_loop(0, 4, sum_x, 0)
    y2_cp = []
    for d in (1, 2, 3):
        y2_send[d - 1] = e1[(y + d) % 4].astype(BF)
        y2_cp.append(send(y2_send.at[d - 1], y2_recv.at[d - 1], y2_ss.at[d - 1], y2_rs.at[d - 1], ydev[d]))
    for copy in y1_cp:
        copy.wait_recv()

    def sum_y(r, _):
        h, x_ = r // 2, r % 2
        v = have(y, h, x_, low)
        for k in range(3):
            v = v + y1_recv[k, h, x_].astype(F32)
        e0[h, x_] = v
        return 0

    lax.fori_loop(0, 4, sum_y, 0)
    x2_cp = []
    for k, (h, x_) in enumerate(xs):
        x2_send[k] = e0[h, x_].astype(BF)
        x2_cp.append(send(x2_send.at[k], x2_recv.at[k], x2_ss.at[k], x2_rs.at[k], xdev[k]))
    for copy in y2_cp + x2_cp:
        copy.wait_recv()
    v0, v1 = e0[xhi, xlo], e1[y]
    for k in range(3):
        v0 = v0 + x2_recv[k].astype(F32)
        v1 = v1 + y2_recv[k].astype(F32)
    dz[0:2] = v0.reshape(2, 2, 16, 128)
    dz[2:4] = v1.reshape(2, 2, 16, 128)
    pl.semaphore_wait(word.at[2], 2)
    m = l // 2
    dl_send[...] = dz[:, 1 - m].astype(BF)
    dl_cp = send(dl_send, dl_recv, dl_ss.at[0], dl_rs.at[0], ldev[2])
    dl_cp.wait_recv()
    dg[...] = dz[:, m] + dl_recv[...].astype(F32)
    dg_cp = []
    for d in (1, 2, 3):
        dg_cp.append(send(dg.at[(g + d) % 4], dg_recv.at[d - 1], dg_ss.at[d - 1], dg_rs.at[d - 1], gdev[d]))
    for copy in dg_cp:
        copy.wait_recv()
    v = dg[g]
    for k in range(3):
        v = v + dg_recv[k]
    dens_ref[...] = v * (1.0 / PAIRS)

    own_copy.wait()
    for copy in o_cp:
        copy.wait_recv()
    for copy in started:
        copy.wait_send()

    slab_copy(s_early).wait_send()
    slab_copy(s_late).wait_send()
    for k in range(4):
        quarter(k).wait_send()


def on_device(b_blocks, occ_energy, vir_energy, coef_vir):
    dma = pltpu.SemaphoreType.DMA
    vm = pltpu.VMEM
    scratch = [
        vm((NV, NAUX), BF),
        vm((STEPS, SLAB, NAUX), BF),
        vm((8, 128), F32),
        vm((STEPS, 8, 128), F32),
        vm((8, 128, NV), BF),
        vm((NV, 128), F32),
        vm((NV, STEPS * SLAB), BF),
        vm((NAO, STEPS * SLAB), BF),
        vm((NAUX, STEPS * SLAB), BF),
        vm((4, 2, 2, 2, 8, 16, 128), F32),
        vm((4, 2, 2, 2, 8, 16, 128), BF),
        vm((4, 2, 2, 2, 8, 16, 128), BF),
        vm((2, 2, 2, 2, 8, 16, 128), BF),
        vm((2, 2, 2, 2, 8, 16, 128), BF),
        vm((3, 2, 2, 4, 16, 128), BF),
        vm((3, 2, 2, 4, 16, 128), BF),
        vm((3, 4, 4, 16, 128), BF),
        vm((3, 4, 4, 16, 128), BF),
        vm((2, 2, 4, 16, 128), F32),
        vm((4, 4, 16, 128), F32),
        vm((3, 4, 16, 128), BF),
        vm((3, 4, 16, 128), BF),
        vm((3, 4, 16, 128), BF),
        vm((3, 4, 16, 128), BF),
        vm((4, 2, 16, 128), F32),
        vm((4, 16, 128), BF),
        vm((4, 16, 128), BF),
        vm((4, 16, 128), F32),
        vm((3, 16, 128), F32),
        vm((1, NV), F32),
        vm((4, 2, 128, NAO), BF),
        vm((4, NV, 256), F32),
        pltpu.SemaphoreType.REGULAR((4,)),
        dma((4,)),
    ]
    for count in (3, 3, 7, 7, 8, 2, 3, 3, 3, 3, 1, 3, 8, 8):
        scratch += [dma((count,)), dma((count,))]
    return pl.pallas_call(
        kernel,
        out_shape=(
            jax.ShapeDtypeStruct((16, 128), F32),
            jax.ShapeDtypeStruct((8, 128, NAO), BF),
        ),
        in_specs=[
            pl.BlockSpec(memory_space=pltpu.HBM),
            pl.BlockSpec(memory_space=pltpu.SMEM),
            pl.BlockSpec(memory_space=pltpu.HBM),
            pl.BlockSpec(memory_space=pltpu.HBM),
        ],
        out_specs=(
            pl.BlockSpec(memory_space=pltpu.VMEM),
            pl.BlockSpec(memory_space=pl.ANY),
        ),
        scratch_shapes=scratch,
        compiler_params=pltpu.CompilerParams(
            collective_id=0, has_side_effects=True, vmem_limit_bytes=50 * 1024 * 1024
        ),
    )(b_blocks, occ_energy, vir_energy.reshape(1, NV), coef_vir)


def solution(mesh):
    return jax.shard_map(
        on_device,
        mesh=mesh,
        in_specs=(P(("wide", "narrow"), None, None), P(("wide", "narrow")), P(), P("narrow", None)),
        out_specs=(P("wide", "narrow"), P("wide", "narrow", None)),
        check_vma=False,
    )
```

```python
import jax
import jax.numpy as jnp
from jax import lax
from jax.experimental import pallas as pl
from jax.experimental.pallas import tpu as pltpu
from jax.sharding import PartitionSpec as P

NV = 1024
NAUX = 1024
NAO = 1024
SLAB = 256
STEPS = 3
PAIRS = 512 * STEPS
MESH = pl.DeviceIdType.MESH
BF = jnp.bfloat16
F32 = jnp.float32
NT = (((1,), (1,)), ((), ()))
Y_ORDER = (2, 1, 3, 0)


def kernel(
    b_hbm,
    occ_ref,
    vir_hbm,
    coef_hbm,
    dens_ref,
    gao_ref,
    b_vm,
    slab,
    e_own,
    e_part,
    cf,
    vcol,
    amp,
    tr,
    st,
    d_own,
    d_send,
    d_recv,
    zp_send,
    zp_recv,
    y1_send,
    y1_recv,
    x1_send,
    x1_recv,
    e0,
    e1,
    x2_send,
    x2_recv,
    y2_send,
    y2_recv,
    dz,
    dl_send,
    dl_recv,
    dg,
    dg_recv,
    vir_ref,
    o_send,
    d_acc,
    word,
    local_sem,
    e_ss,
    e_rs,
    s_ss,
    s_rs,
    c_ss,
    c_rs,
    f_ss,
    f_rs,
    dc_ss,
    dc_rs,
    zp_ss,
    zp_rs,
    y1_ss,
    y1_rs,
    x1_ss,
    x1_rs,
    x2_ss,
    x2_rs,
    y2_ss,
    y2_rs,
    dl_ss,
    dl_rs,
    dg_ss,
    dg_rs,
    o_ss,
    o_rs,
    r_ss,
    r_rs,
):
    w = lax.axis_index("wide")
    n = lax.axis_index("narrow")
    z, xlo, core = w // 4, (w // 2) % 2, w % 2
    xhi, y = n // 4, n % 4
    g, l = z // 4, z % 4

    def at(z_, xlo_, core_, xhi_, y_):
        return (z_ * 4 + xlo_ * 2 + core_, xhi_ * 4 + y_)

    started = []

    def send(src, dst, ss, rs, dev):
        copy = pltpu.make_async_remote_copy(
            src_ref=src, dst_ref=dst, send_sem=ss, recv_sem=rs, device_id=dev, device_id_type=MESH
        )
        copy.start()
        started.append(copy)
        return copy

    other = at(z, xlo, 1 - core, xhi, y)
    across = at(z, 1 - xlo, core, 1 - xhi, y)
    ydev = [None] + [at(z, xlo, core, xhi, (y + d) % 4) for d in (1, 2, 3)]
    xdev = [
        at(z, xlo, core, 1 - xhi, y),
        at(z, 1 - xlo, core, xhi, y),
        across,
    ]
    ldev = [None] + [at(g * 4 + (l + d) % 4, xlo, core, xhi, y) for d in (1, 2, 3)]
    gdev = [None] + [at((g + d) % 4 * 4 + l, xlo, core, xhi, y) for d in (1, 2, 3)]

    barrier = pltpu.get_barrier_semaphore()
    greet = [((w + 64 - s) % 64, n) for s in (1, 2, 3, 4)]
    greet += [((w + 2) % 64, n), ((w + 4) % 64, n)]
    greet += [other] + xdev + ydev[1:]
    for dev in greet:
        pl.semaphore_signal(barrier, inc=1, device_id=dev, device_id_type=MESH)

    load_b = pltpu.make_async_copy(b_hbm.at[0], b_vm, local_sem.at[0])
    load_b.start()
    load_c = pltpu.make_async_copy(coef_hbm, cf.at[n], local_sem.at[1])
    load_c.start()
    load_v = pltpu.make_async_copy(vir_hbm, vir_ref, local_sem.at[3])
    load_v.start()
    e_own[...] = jnp.full((8, 128), occ_ref[0], F32)

    pl.semaphore_wait(barrier, len(greet))

    def pass_word(k, devs):
        for dev in devs:
            pl.semaphore_signal(word.at[k], inc=1, device_id=dev, device_id_type=MESH)

    def along(d):
        return [((w + 4 * d) % 64, n), ((w + 64 - 4 * d) % 64, n)]

    e_cp = []
    for s in range(STEPS):
        dev = ((w + s + 1) % 64, n)
        e_cp.append(send(e_own, e_part.at[s], e_ss.at[s], e_rs.at[s], dev))
    s_early, s_late = core * 2, 2 - core * 2
    r_early, r_late = 2 - core * 2, core * 2

    def slab_copy(s):
        return pltpu.make_async_remote_copy(
            src_ref=b_hbm.at[0, pl.ds(pl.multiple_of(s * SLAB, SLAB), SLAB)],
            dst_ref=slab.at[s],
            send_sem=s_ss.at[s],
            recv_sem=s_rs.at[s],
            device_id=((w + s + 1) % 64, n),
            device_id_type=MESH,
        )

    def quarter(k):
        return pltpu.make_async_remote_copy(
            src_ref=b_hbm.at[0, pl.ds(SLAB + k * 64, 64)],
            dst_ref=slab.at[1, pl.ds(k * 64, 64)],
            send_sem=r_ss.at[k],
            recv_sem=r_rs.at[4 + k],
            device_id=((w + 2) % 64, n),
            device_id_type=MESH,
        )

    slab_copy(s_early).start()
    for k in range(4):
        quarter(k).start()
    slab_copy(s_late).start()
    pass_word(0, along(1))
    pass_word(3, [xdev[0]])

    half = pl.ds(pl.multiple_of(core * 64, 64), 64)
    mine = coef_hbm.at[half]
    c_cp = [send(mine, cf.at[n, half], c_ss.at[0], c_rs.at[0], across)]
    for d in (1, 2, 3):
        c_cp.append(send(mine, cf.at[n, half], c_ss.at[d], c_rs.at[d], ydev[d]))

    load_v.wait()
    for k in range(8):
        row = vir_ref[:, k * 128 : (k + 1) * 128]
        vcol[k * 128 : (k + 1) * 128, :] = jnp.broadcast_to(row, (128, 128)).T

    c_cp[0].wait_recv()
    far = cf.at[(1 - xhi) * 4 + y, half]
    for d in (1, 2, 3):
        c_cp.append(send(far, far, c_ss.at[3 + d], c_rs.at[3 + d], ydev[d]))
    f_cp = [send(far, far, f_ss.at[0], f_rs.at[0], other)]
    pl.semaphore_wait(word.at[0], 2)
    pass_word(1, along(2))
    for d in (1, 2, 3):
        c_cp[d].wait_recv()
        piece = cf.at[xhi * 4 + (y + 4 - d) % 4, half]
        f_cp.append(send(piece, piece, f_ss.at[d], f_rs.at[d], other))
    pl.semaphore_wait(word.at[1], 2)
    pass_word(2, along(4))
    load_b.wait()

    def couple(slot, s):
        if slot == 0:
            for copy in e_cp:
                copy.wait_recv()
        if slot == 1:
            for k in range(4):
                quarter(k).wait_recv()
        else:
            slab_copy(s).wait_recv()
        e_sum = (e_own[...] + e_part[s])[0:1, 0:1]
        e_slab = vir_ref[:, pl.ds(pl.multiple_of(s * SLAB, SLAB), SLAB)]
        c = lax.dot_general(b_vm[...], slab[s], NT, preferred_element_type=F32)
        denom = (e_sum - vcol[:, 0:1]) - e_slab
        amp[:, slot * SLAB : (slot + 1) * SLAB] = (c / denom).astype(BF)

    def transform(slot, s):
        cols = slice(slot * SLAB, (slot + 1) * SLAB)
        for k in range(4):
            st[k * 256 : (k + 1) * 256, cols] = slab[s, :, k * 256 : (k + 1) * 256].T

        t = jnp.dot(cf[...].reshape(NAO, NV), amp[:, cols], preferred_element_type=F32)
        tr[:, cols] = t.astype(BF)

    couple(0, r_early)

    for d in (1, 2, 3):
        c_cp[3 + d].wait_recv()
        piece = cf.at[(1 - xhi) * 4 + (y + 4 - d) % 4, half]
        f_cp.append(send(piece, piece, f_ss.at[3 + d], f_rs.at[3 + d], other))
    load_c.wait()
    for copy in f_cp:
        copy.wait_recv()

    transform(0, r_early)
    couple(1, 1)
    transform(1, 1)

    def columns(d):
        y_ = (y + d) % 4
        return (y_, pl.ds(pl.multiple_of(y_ * 128, 128), 128), pl.ds(pl.multiple_of(512 + y_ * 128, 128), 128))

    for q, d in enumerate(Y_ORDER):
        _, lo, hi = columns(d)
        right = jnp.concatenate([amp[lo, : 2 * SLAB], amp[hi, : 2 * SLAB]], axis=0)
        d_acc[q] = lax.dot_general(amp[:, : 2 * SLAB], right, NT, preferred_element_type=F32)
    couple(2, r_late)

    transform(2, r_late)
    pl.semaphore_wait(word.at[3], 1)
    o_cp = []

    def blocks(q):
        d = Y_ORDER[q]
        y_, lo, hi = columns(d)
        left = jnp.concatenate([st[lo, :], st[hi, :]], axis=0)
        v = lax.dot_general(left, tr[...], NT, preferred_element_type=F32).astype(BF)
        o_send[q, 0] = v[:128]
        o_send[q, 1] = v[128:]
        i = 2 * q
        o_cp.append(
            send(o_send.at[q, 1 - xhi], gao_ref.at[n], o_ss.at[i], o_rs.at[i], at(z, xlo, core, 1 - xhi, y_))
        )
        if d:
            i = i + 1
            o_cp.append(send(o_send.at[q, xhi], gao_ref.at[n], o_ss.at[i], o_rs.at[i], at(z, xlo, core, xhi, y_)))

    for q in range(4):
        blocks(q)
    own_copy = pltpu.make_async_copy(o_send.at[3, xhi], gao_ref.at[n], local_sem.at[2])
    own_copy.start()
    top, low = pl.ds(4, 4), pl.ds(0, 4)
    par = z % 2
    dt_cp, dc_cp = [], []
    for q, d in enumerate(Y_ORDER):
        y_, lo, hi = columns(d)
        right = jnp.concatenate([amp[lo, 2 * SLAB :], amp[hi, 2 * SLAB :]], axis=0)
        v = d_acc[q] + lax.dot_general(amp[:, 2 * SLAB :], right, NT, preferred_element_type=F32)
        v = v.reshape(8, 2, 2, 2, 16, 256)
        v0, v1 = v[:, :, :, 0], v[:, :, :, 1]
        keep = jnp.where(core == 0, v0, v1)
        give = jnp.where(core == 0, v1, v0).astype(BF)
        for h in range(2):
            for x_ in range(2):
                for p in range(2):
                    d_own[y_, h, x_, p] = keep[:, p, x_, :, h * 128 : (h + 1) * 128]
                    d_send[y_, h, x_, p] = give[:, p, x_, :, h * 128 : (h + 1) * 128]
        for i, p, cps in ((2 * q, 1 - par, dt_cp), (2 * q + 1, par, dc_cp)):
            cps.append(send(d_send.at[y_, :, :, p], d_recv.at[y_, :, :, p], dc_ss.at[i], dc_rs.at[i], other))


    for copy in dt_cp:
        copy.wait_recv()
    step = 1 - 2 * par
    zdev = [((w + 64 + 4 * step) % 64, n), ((w + 64 - 4 * step) % 64, n)]
    zp_cp = []
    for k in range(2):

        def add(r, _):
            h, x_ = r // 2, r % 2
            for i in range(2):
                v = d_own[2 * k + i, h, x_, 1 - par] + d_recv[2 * k + i, h, x_, 1 - par].astype(F32)
                zp_send[k, i, h, x_] = v.astype(BF)
            return 0

        lax.fori_loop(0, 4, add, 0)
        zp_cp.append(send(zp_send.at[k], zp_recv.at[k], zp_ss.at[k], zp_rs.at[k], zdev[k]))

    for copy in dc_cp + zp_cp:
        copy.wait_recv()

    def have(y_, h, x_, part):
        v = d_own[y_, h, x_, par, part] + d_recv[y_, h, x_, par, part].astype(F32)
        return v + zp_recv[y_ // 2, y_ % 2, h, x_, part].astype(F32)

    xs = ((1 - xhi, xlo), (xhi, 1 - xlo), (1 - xhi, 1 - xlo))
    x1_cp, y1_cp = [], []
    for k, (h, x_) in enumerate(xs):

        def add(r, _):
            x1_send[k, r] = have(r, h, x_, top).astype(BF)
            return 0

        lax.fori_loop(0, 4, add, 0)
        x1_cp.append(send(x1_send.at[k], x1_recv.at[k], x1_ss.at[k], x1_rs.at[k], xdev[k]))
    for q, d in enumerate(Y_ORDER[:3]):

        def add(r, _):
            y1_send[q, r // 2, r % 2] = have((y + d) % 4, r // 2, r % 2, low).astype(BF)
            return 0

        lax.fori_loop(0, 4, add, 0)
        y1_cp.append(send(y1_send.at[q], y1_recv.at[q], y1_ss.at[q], y1_rs.at[q], ydev[d]))

    for copy in x1_cp:
        copy.wait_recv()

    def sum_x(r, _):
        v = have(r, xhi, xlo, top)
        for k in range(3):
            v = v + x1_recv[k, r].astype(F32)
        e1[r] = v
        return 0

    lax.fori_loop(0, 4, sum_x, 0)
    y2_cp = []
    for d in (1, 2, 3):
        y2_send[d - 1] = e1[(y + d) % 4].astype(BF)
        y2_cp.append(send(y2_send.at[d - 1], y2_recv.at[d - 1], y2_ss.at[d - 1], y2_rs.at[d - 1], ydev[d]))
    for copy in y1_cp:
        copy.wait_recv()

    def sum_y(r, _):
        h, x_ = r // 2, r % 2
        v = have(y, h, x_, low)
        for k in range(3):
            v = v + y1_recv[k, h, x_].astype(F32)
        e0[h, x_] = v
        return 0

    lax.fori_loop(0, 4, sum_y, 0)
    x2_cp = []
    for k, (h, x_) in enumerate(xs):
        x2_send[k] = e0[h, x_].astype(BF)
        x2_cp.append(send(x2_send.at[k], x2_recv.at[k], x2_ss.at[k], x2_rs.at[k], xdev[k]))
    for copy in y2_cp + x2_cp:
        copy.wait_recv()
    v0, v1 = e0[xhi, xlo], e1[y]
    for k in range(3):
        v0 = v0 + x2_recv[k].astype(F32)
        v1 = v1 + y2_recv[k].astype(F32)
    dz[0:2] = v0.reshape(2, 2, 16, 128)
    dz[2:4] = v1.reshape(2, 2, 16, 128)
    pl.semaphore_wait(word.at[2], 2)
    m = l // 2
    dl_send[...] = dz[:, 1 - m].astype(BF)
    dl_cp = send(dl_send, dl_recv, dl_ss.at[0], dl_rs.at[0], ldev[2])
    dl_cp.wait_recv()
    dg[...] = dz[:, m] + dl_recv[...].astype(F32)
    dg_cp = []
    for d in (1, 2, 3):
        dg_cp.append(send(dg.at[(g + d) % 4], dg_recv.at[d - 1], dg_ss.at[d - 1], dg_rs.at[d - 1], gdev[d]))
    for copy in dg_cp:
        copy.wait_recv()
    v = dg[g]
    for k in range(3):
        v = v + dg_recv[k]
    dens_ref[...] = v * (1.0 / PAIRS)

    own_copy.wait()
    for copy in o_cp:
        copy.wait_recv()
    for copy in started:
        copy.wait_send()

    slab_copy(s_early).wait_send()
    slab_copy(s_late).wait_send()
    for k in range(4):
        quarter(k).wait_send()


def on_device(b_blocks, occ_energy, vir_energy, coef_vir):
    dma = pltpu.SemaphoreType.DMA
    vm = pltpu.VMEM
    scratch = [
        vm((NV, NAUX), BF),
        vm((STEPS, SLAB, NAUX), BF),
        vm((8, 128), F32),
        vm((STEPS, 8, 128), F32),
        vm((8, 128, NV), BF),
        vm((NV, 128), F32),
        vm((NV, STEPS * SLAB), BF),
        vm((NAO, STEPS * SLAB), BF),
        vm((NAUX, STEPS * SLAB), BF),
        vm((4, 2, 2, 2, 8, 16, 128), F32),
        vm((4, 2, 2, 2, 8, 16, 128), BF),
        vm((4, 2, 2, 2, 8, 16, 128), BF),
        vm((2, 2, 2, 2, 8, 16, 128), BF),
        vm((2, 2, 2, 2, 8, 16, 128), BF),
        vm((3, 2, 2, 4, 16, 128), BF),
        vm((3, 2, 2, 4, 16, 128), BF),
        vm((3, 4, 4, 16, 128), BF),
        vm((3, 4, 4, 16, 128), BF),
        vm((2, 2, 4, 16, 128), F32),
        vm((4, 4, 16, 128), F32),
        vm((3, 4, 16, 128), BF),
        vm((3, 4, 16, 128), BF),
        vm((3, 4, 16, 128), BF),
        vm((3, 4, 16, 128), BF),
        vm((4, 2, 16, 128), F32),
        vm((4, 16, 128), BF),
        vm((4, 16, 128), BF),
        vm((4, 16, 128), F32),
        vm((3, 16, 128), F32),
        vm((1, NV), F32),
        vm((4, 2, 128, NAO), BF),
        vm((4, NV, 256), F32),
        pltpu.SemaphoreType.REGULAR((4,)),
        dma((4,)),
    ]
    for count in (3, 3, 7, 7, 8, 2, 3, 3, 3, 3, 1, 3, 8, 8):
        scratch += [dma((count,)), dma((count,))]
    return pl.pallas_call(
        kernel,
        out_shape=(
            jax.ShapeDtypeStruct((16, 128), F32),
            jax.ShapeDtypeStruct((8, 128, NAO), BF),
        ),
        in_specs=[
            pl.BlockSpec(memory_space=pltpu.HBM),
            pl.BlockSpec(memory_space=pltpu.SMEM),
            pl.BlockSpec(memory_space=pltpu.HBM),
            pl.BlockSpec(memory_space=pltpu.HBM),
        ],
        out_specs=(
            pl.BlockSpec(memory_space=pltpu.VMEM),
            pl.BlockSpec(memory_space=pl.ANY),
        ),
        scratch_shapes=scratch,
        compiler_params=pltpu.CompilerParams(
            collective_id=0, has_side_effects=True, vmem_limit_bytes=50 * 1024 * 1024
        ),
    )(b_blocks, occ_energy, vir_energy.reshape(1, NV), coef_vir)


def solution(mesh):
    return jax.shard_map(
        on_device,
        mesh=mesh,
        in_specs=(P(("wide", "narrow"), None, None), P(("wide", "narrow")), P(), P("narrow", None)),
        out_specs=(P("wide", "narrow"), P("wide", "narrow", None)),
        check_vma=False,
    )
```
